32 devices in a mesh: ctx: 8 (over z, y), wa: 4 (over x, core).
Axes of the slice: x: 2, y: 2, z: 4, core: 2. Of those that a mesh axis runs over, the one named last changes fastest.
Arguments:
- tokens: bfloat16 [6144, 576], P(('ctx', 'wa')), may hold values from -6 to 6
- segment_ids: int32 [6144], replicated, may hold values from 0 to 5, as said below
- w_query: bfloat16 [576, 576], P('wa'), may hold values from -0.5 to 0.5
- w_key: bfloat16 [576, 192], P('wa'), may hold values from -0.25 to 0.25
- w_value: bfloat16 [576, 192], P('wa'), may hold values from -0.25 to 0.25
- w_out: bfloat16 [576, 576], P('wa'), may hold values from -1.5 to 1.5
- w_gate: bfloat16 [576, 1536], P('wa'), may hold values from -0.25 to 0.25
- w_up: bfloat16 [576, 1536], P('wa'), may hold values from -0.25 to 0.25
- w_down: bfloat16 [1536, 576], P('wa'), may hold values from -0.15625 to 0.15625
- gain_attn: bfloat16 [576], P('wa'), may hold values from 0.5 to 1.5
- gain_ffn: bfloat16 [576], P('wa'), may hold values from 0.5 to 1.5
- cotangent: bfloat16 [6144, 576], P(('ctx', 'wa')), may hold values from -6 to 6
Outputs:
- output: bfloat16 [6144, 576], P(('ctx', 'wa'))
- grad_tokens: bfloat16 [6144, 576], P(('ctx', 'wa'))
- grad_query: float32 [576, 576], P('wa')
- grad_key: float32 [576, 192], P('wa')
- grad_value: float32 [576, 192], P('wa')
- grad_out: float32 [576, 576], P('wa')
- grad_gate: float32 [576, 1536], P('wa')
- grad_up: float32 [576, 1536], P('wa')
- grad_down: float32 [1536, 576], P('wa')
- grad_gain_attn: float32 [576], P('wa')
- grad_gain_ffn: float32 [576], P('wa')
The draws below stay inside these ranges and needn't reach their ends.
Inputs may be any that keep to these rules, and one draw needn't show every extreme that they name: `segment_ids`: ids never decrease along the tokens, and no document (the tokens of one id) has tokens on both sides of position 3072.
All inputs are finite; a program needn't handle non-finite values.
Results may differ from the reference program's by a relative error of at most 0.02.
Values may be sent and summed in bfloat16 or wider, within the bound.
A program may use at most 64 MiB of HBM per device.

```python
import math
import jax
import jax.numpy as jnp
from jax import lax

D = 576
HEADS = 9
KV_HEADS = 3
HEAD_DIM = 64
FF = 1536
BLOCK = 768
HALF = 3072
TOKENS = 6144


def draw_segment_ids(key, part):
    key = jax.random.fold_in(key, 7)
    head_key, tail_key = jax.random.split(key)
    head_lengths = jax.random.randint(head_key, (2,), 1, BLOCK)
    tail_lengths = jax.random.randint(tail_key, (2,), 1, BLOCK)
    places = jnp.arange(HALF, dtype=jnp.int32)
    pieces = []
    for half_index in range(2):
        after_head = (places >= head_lengths[half_index]).astype(jnp.int32)
        after_body = (places >= HALF - tail_lengths[half_index]).astype(jnp.int32)
        pieces.append(3 * half_index + after_head + after_body)
    return jnp.concatenate(pieces).astype(jnp.int32)


def levels(key, shape, cuts, smallest, high):
    level, own = 1.0, jax.random.fold_in(key, 6)
    for position, blocks in cuts:
        draws = jnp.exp(jax.random.uniform(jax.random.fold_in(own, position), (blocks,), jnp.float32, smallest / len(cuts), high / len(cuts)))
        level = level * jnp.repeat(draws, shape[position] // blocks).reshape([-1 if axis == position else 1 for axis in range(len(shape))])
    return level


def bell_draw(own_key, shape, spread, most, cuts=(), kind=jnp.bfloat16):
    drawn = spread * jax.random.normal(own_key, shape, jnp.float32)
    if cuts:
        drawn = drawn * levels(own_key, shape, cuts, -0.22, 0.18)
    return jnp.clip(drawn, -most, most).astype(kind)


def setup_inputs(seed: int = 0) -> dict:
    keys = jax.random.split(jax.random.key(seed), 13)
    return {
        "tokens": bell_draw(keys[0], (TOKENS, D), 1.0, 6.0, ((0, 32),)),
        "segment_ids": draw_segment_ids(jax.random.fold_in(keys[12], 71), 0),
        "w_query": bell_draw(keys[2], (D, D), (D // 4) ** -0.5, 0.5, ((0, 4),)),
        "w_key": bell_draw(keys[3], (D, KV_HEADS * HEAD_DIM), D ** -0.5, 0.25, ((0, 4),)),
        "w_value": bell_draw(keys[4], (D, KV_HEADS * HEAD_DIM), D ** -0.5, 0.25, ((0, 4),)),
        "w_out": bell_draw(keys[5], (D, D), (D // 36) ** -0.5, 1.5, ((0, 4),)),
        "w_gate": bell_draw(keys[6], (D, FF), D ** -0.5, 0.25, ((0, 4),)),
        "w_up": bell_draw(keys[7], (D, FF), D ** -0.5, 0.25, ((0, 4),)),
        "w_down": bell_draw(keys[8], (FF, D), FF ** -0.5, 0.15625, ((0, 4),)),
        "gain_attn": jnp.clip(1.0 + 0.1 * jax.random.normal(keys[9], (D,), jnp.float32), 0.5, 1.5).astype(jnp.bfloat16),
        "gain_ffn": jnp.clip(1.0 + 0.1 * jax.random.normal(keys[10], (D,), jnp.float32), 0.5, 1.5).astype(jnp.bfloat16),
        "cotangent": bell_draw(keys[11], (TOKENS, D), 1.0, 6.0, ((0, 32),)),
    }


EPSILON = 1e-05
ROPE_BASE = 100000.0
MASKED_SCORE = -1e+30

@jax.custom_vjp
def low(v):
    return lax.optimization_barrier(v.astype(jnp.bfloat16)).astype(jnp.float32)

@jax.custom_vjp
def low_back(v):
    return v

def low_keep(v):
    return (low(v), None)

def low_pass(kept, grad):
    return (grad,)

def back_keep(v):
    return (v, None)

def back_low(kept, grad):
    return (low(grad),)
low.defvjp(low_keep, low_pass)
low_back.defvjp(back_keep, back_low)

def rms_scale(vector):
    return lax.rsqrt(lax.optimization_barrier(jnp.mean(vector * vector, axis=-1, keepdims=True)) + EPSILON)

def rotate(tensor, cosine_table, sine_table):
    half_dim = tensor.shape[-1] // 2
    front_part = tensor[..., :half_dim]
    back_part = tensor[..., half_dim:]
    return jnp.concatenate([front_part * cosine_table - back_part * sine_table, back_part * cosine_table + front_part * sine_table], axis=-1)

def rope_tables(positions, head_size):
    half_dim = head_size // 2
    frequency = ROPE_BASE ** (-(jnp.arange(half_dim, dtype=jnp.float32) * 2.0) / head_size)
    angle_table = positions.astype(jnp.float32)[:, None] * frequency[None, :]
    return (jnp.cos(angle_table)[:, None, :], jnp.sin(angle_table)[:, None, :])

def layer_forward(inputs, w_query, w_key, w_value, w_out, w_gate, w_up, w_down, gain_attn, gain_ffn, segment_ids, cosine_table, sine_table):
    highest = lax.Precision.HIGHEST
    token_count = inputs.shape[0]
    group_size = HEADS // KV_HEADS
    normed = low(inputs * rms_scale(inputs) * gain_attn)
    query_pre = low_back(jnp.dot(normed, w_query, precision=highest)).reshape(token_count, HEADS, HEAD_DIM)
    key_pre = low_back(jnp.dot(normed, w_key, precision=highest)).reshape(token_count, KV_HEADS, HEAD_DIM)
    values = low(low_back(jnp.dot(normed, w_value, precision=highest))).reshape(token_count, KV_HEADS, HEAD_DIM)
    query = low(rotate(query_pre, cosine_table, sine_table))
    key_rot = low(rotate(key_pre, cosine_table, sine_table))
    key_all = jnp.repeat(key_rot, group_size, axis=1)
    value_all = jnp.repeat(values, group_size, axis=1)
    block_width = math.gcd(HALF, 512)
    starts = jnp.arange(token_count // block_width, dtype=jnp.int32) * block_width

    def query_block(start):
        half_start = start // HALF * HALF
        query_rows = lax.dynamic_slice_in_dim(query, start, block_width, 0)
        key_rows = lax.dynamic_slice_in_dim(key_all, half_start, HALF, 0)
        value_rows = lax.dynamic_slice_in_dim(value_all, half_start, HALF, 0)
        query_segs = lax.dynamic_slice_in_dim(segment_ids, start, block_width, 0)
        key_segs = lax.dynamic_slice_in_dim(segment_ids, half_start, HALF, 0)
        query_ids = start + jnp.arange(block_width, dtype=jnp.int32)
        key_ids = half_start + jnp.arange(HALF, dtype=jnp.int32)
        allowed_pairs = (query_segs[:, None] == key_segs[None, :]) & (key_ids[None, :] <= query_ids[:, None])
        scores = low_back(jnp.einsum('qhd,khd->hqk', query_rows, key_rows, precision=highest) * HEAD_DIM ** (-0.5))
        scores = jnp.where(allowed_pairs[None], scores, MASKED_SCORE)
        maxima = lax.optimization_barrier(jnp.max(scores, axis=-1, keepdims=True))
        exponent = jnp.exp(scores - maxima)
        attention_weights = low(exponent / lax.optimization_barrier(jnp.sum(exponent, axis=-1, keepdims=True)))
        return jnp.einsum('hqk,khd->qhd', attention_weights, value_rows, precision=highest)
    attended = lax.map(jax.checkpoint(query_block), starts)
    attention = low(low_back(attended.reshape(token_count, HEADS * HEAD_DIM)))
    residual = inputs + low_back(jnp.dot(attention, w_out, precision=highest))
    normed_two = low(residual * rms_scale(residual) * gain_ffn)
    gate_pre = low_back(jnp.dot(normed_two, w_gate, precision=highest))
    up_pre = low_back(jnp.dot(normed_two, w_up, precision=highest))
    hidden_act = low(jax.nn.silu(gate_pre) * up_pre)
    return residual + low_back(jnp.dot(hidden_act, w_down, precision=highest))

def reference(tokens, segment_ids, w_query, w_key, w_value, w_out, w_gate, w_up, w_down, gain_attn, gain_ffn, cotangent):
    token_ids = jnp.arange(TOKENS, dtype=jnp.int32)
    positions = token_ids - jnp.searchsorted(segment_ids, segment_ids, side='left').astype(jnp.int32)
    cosine_table, sine_table = rope_tables(positions, HEAD_DIM)

    def forward(inputs, query_w, key_w, value_w, out_w, gate_w, up_w, down_w, gain_one, gain_two):
        return layer_forward(inputs, query_w, key_w, value_w, out_w, gate_w, up_w, down_w, gain_one, gain_two, segment_ids, cosine_table, sine_table)
    result, pullback = jax.vjp(forward, tokens.astype(jnp.float32), w_query.astype(jnp.float32), w_key.astype(jnp.float32), w_value.astype(jnp.float32), w_out.astype(jnp.float32), w_gate.astype(jnp.float32), w_up.astype(jnp.float32), w_down.astype(jnp.float32), gain_attn.astype(jnp.float32), gain_ffn.astype(jnp.float32))
    gradients = pullback(cotangent.astype(jnp.float32))
    return (result.astype(jnp.bfloat16), gradients[0].astype(jnp.bfloat16), gradients[1], gradients[2], gradients[3], gradients[4], gradients[5], gradients[6], gradients[7], gradients[8], gradients[9])
```

```python
import jax
import jax.numpy as jnp
from jax import lax
from jax.sharding import PartitionSpec as P

HEADS = 9
KV_HEADS = 3
HEAD_DIM = 64


EPSILON = 1e-05
ROPE_BASE = 100000.0
MASKED_SCORE = -1e30


def passed_along(shard, axis, by):
    count = lax.axis_size(axis)
    pairs = [(i, i + by) for i in range(count) if 0 <= i + by < count]
    return lax.ppermute(shard, axis, pairs)


def shifted(block, axis, distance):
    devices = range(lax.axis_size(axis))
    route = [((i - distance) % len(devices), i) for i in devices]
    return lax.ppermute(block, axis, route)


def rms_scale(vector):
    return lax.rsqrt(jnp.mean(vector * vector, axis=-1, keepdims=True) + EPSILON)


def rotate(tensor, cosine_table, sine_table):
    half_dim = tensor.shape[-1] // 2
    front_part = tensor[..., :half_dim]
    back_part = tensor[..., half_dim:]
    return jnp.concatenate(
        [
            front_part * cosine_table - back_part * sine_table,
            back_part * cosine_table + front_part * sine_table,
        ],
        axis=-1,
    )


def unrotate(gradient, cosine_table, sine_table):
    half_dim = gradient.shape[-1] // 2
    front_part = gradient[..., :half_dim]
    back_part = gradient[..., half_dim:]
    return jnp.concatenate(
        [
            front_part * cosine_table + back_part * sine_table,
            back_part * cosine_table - front_part * sine_table,
        ],
        axis=-1,
    )


def rope_tables(positions, head_size):
    half_dim = head_size // 2
    frequency = ROPE_BASE ** (-(jnp.arange(half_dim, dtype=jnp.float32) * 2.0) / head_size)
    angle_table = positions.astype(jnp.float32)[:, None] * frequency[None, :]
    return (jnp.cos(angle_table)[:, None, :], jnp.sin(angle_table)[:, None, :])


def norm_back(gradient, vector, row_scale, gain_row):
    gain_grad = jnp.sum(gradient * (vector * row_scale), axis=0)
    scaled = gradient * gain_row
    input_grad = row_scale * scaled - row_scale * row_scale * row_scale * vector * jnp.mean(
        scaled * vector, axis=-1, keepdims=True
    )
    return (input_grad, gain_grad)


def on_device(
    tokens,
    segment_ids,
    w_query,
    w_key,
    w_value,
    w_out,
    w_gate,
    w_up,
    w_down,
    gain_attn,
    gain_ffn,
    cotangent,
):
    row_count = tokens.shape[0]
    ctx_count = lax.axis_size("ctx")
    wa_count = lax.axis_size("wa")
    ctx_index = lax.axis_index("ctx")
    wa_index = lax.axis_index("wa")
    block_rows = row_count * wa_count
    half_blocks = ctx_count // 2
    group_size = HEADS // KV_HEADS
    kv_width = KV_HEADS * HEAD_DIM
    score_scale = HEAD_DIM ** (-0.5)
    row_start = (ctx_index * wa_count + wa_index) * row_count
    widths = tuple(
        w.shape[1] for w in (w_query, w_key, w_value, w_out, w_gate, w_up)
    )
    early = jnp.concatenate(
        [w_query, w_key, w_value, gain_attn[:, None], gain_ffn[:, None]], axis=1
    )
    early = lax.all_gather(early, "wa", axis=0, tiled=True)
    late = lax.all_gather(
        jnp.concatenate([w_out, w_gate, w_up], axis=1), "wa", axis=0, tiled=True
    )
    down_full = lax.all_gather(w_down, "wa", axis=0, tiled=True)
    ends = (widths[0], widths[0] + widths[1], widths[0] + widths[1] + widths[2])
    query_full = early[:, : ends[0]]
    key_full = early[:, ends[0] : ends[1]]
    value_full = early[:, ends[1] : ends[2]]
    gain_one = early[:, ends[2]]
    gain_two = early[:, ends[2] + 1]
    out_full = late[:, : widths[3]]
    gate_full = late[:, widths[3] : widths[3] + widths[4]]
    up_full = late[:, widths[3] + widths[4] :]
    query_ids = row_start + jnp.arange(row_count, dtype=jnp.int32)
    query_segs = lax.dynamic_slice_in_dim(segment_ids, row_start, row_count)
    positions = query_ids - jnp.searchsorted(segment_ids, query_segs, side="left")
    cosine_table, sine_table = rope_tables(positions, HEAD_DIM)
    inputs = tokens.astype(jnp.float32)
    scale_one = rms_scale(inputs)
    gain_first = gain_one.astype(jnp.float32)
    normed = (inputs * scale_one * gain_first).astype(jnp.bfloat16)
    query_pre = jnp.dot(normed, query_full, preferred_element_type=jnp.float32).reshape(
        row_count, HEADS, HEAD_DIM
    )
    key_pre = jnp.dot(normed, key_full, preferred_element_type=jnp.float32).reshape(
        row_count, KV_HEADS, HEAD_DIM
    )
    value_low = jnp.dot(normed, value_full, preferred_element_type=jnp.float32).astype(jnp.bfloat16)
    query_low = rotate(query_pre, cosine_table, sine_table).astype(jnp.bfloat16)
    key_low = (
        rotate(key_pre, cosine_table, sine_table).astype(jnp.bfloat16).reshape(row_count, kv_width)
    )
    query_grid = query_low.reshape(row_count, KV_HEADS, group_size, HEAD_DIM).transpose(1, 2, 0, 3)
    own_rows = jnp.concatenate([key_low, value_low], axis=1)
    whole_half = half_blocks <= 4
    if whole_half:
        members = half_blocks * wa_count
        halves = [list(range(members)), list(range(members, 2 * members))]
        half_start = (ctx_index // half_blocks) * (half_blocks * block_rows)
        half_rows = half_blocks * block_rows
        half_kv = lax.all_gather(
            own_rows, ("ctx", "wa"), axis=0, tiled=True, axis_index_groups=halves
        )
        half_keys = half_kv[:, :kv_width].reshape(half_rows, KV_HEADS, HEAD_DIM)
        half_values = half_kv[:, kv_width:].reshape(half_rows, KV_HEADS, HEAD_DIM)
        half_ids = half_start + jnp.arange(half_rows, dtype=jnp.int32)
        half_segs = lax.dynamic_slice_in_dim(segment_ids, half_start, half_rows)
        half_allowed = (query_segs[:, None] == half_segs[None, :]) & (
            half_ids[None, :] <= query_ids[:, None]
        )
    else:
        own_block = lax.all_gather(own_rows, "wa", axis=0, tiled=True)

    def half_scores(group):
        raw = (
            jnp.einsum(
                "ird,kd->irk",
                query_grid[group],
                half_keys[:, group],
                preferred_element_type=jnp.float32,
            )
            * score_scale
        )
        return jnp.where(half_allowed[None], raw, MASKED_SCORE)

    def half_forward(group):
        masked = half_scores(group)
        top = jnp.max(masked, axis=-1)
        exponent = jnp.exp(masked - top[..., None])
        total = jnp.sum(exponent, axis=-1)
        summed = jnp.einsum(
            "irk,kd->ird",
            exponent.astype(jnp.bfloat16),
            half_values[:, group],
            preferred_element_type=jnp.float32,
        )
        return (top, total, summed)

    own_start = ctx_index * block_rows

    def block_start(offset):
        return jnp.mod(ctx_index - offset, ctx_count) * block_rows

    def scores_of(kv_block, key_start):
        key_rows = kv_block[:, :kv_width].reshape(block_rows, KV_HEADS, HEAD_DIM)
        value_rows = kv_block[:, kv_width:].reshape(block_rows, KV_HEADS, HEAD_DIM)
        raw_scores = (
            jnp.einsum("gird,kgd->girk", query_grid, key_rows, preferred_element_type=jnp.float32)
            * score_scale
        )
        key_ids = key_start + jnp.arange(block_rows, dtype=jnp.int32)
        key_segs = lax.dynamic_slice_in_dim(segment_ids, key_start, block_rows)
        allowed_pairs = (query_segs[:, None] == key_segs[None, :]) & (
            key_ids[None, :] <= query_ids[:, None]
        )
        return (jnp.where(allowed_pairs, raw_scores, MASKED_SCORE), key_rows, value_rows)

    def attend_block(running, kv_block, key_start):
        maxima, totals, summed = running
        masked, key_rows, value_rows = scores_of(kv_block, key_start)
        new_max = jnp.maximum(maxima, jnp.max(masked, axis=-1))
        factor = jnp.exp(maxima - new_max)
        exponent = jnp.exp(masked - new_max[..., None])
        totals = totals * factor + jnp.sum(exponent, axis=-1)
        summed = summed * factor[..., None] + jnp.einsum(
            "girk,kgd->gird",
            exponent.astype(jnp.bfloat16),
            value_rows,
            preferred_element_type=jnp.float32,
        )
        return (new_max, totals, summed)

    if whole_half:
        parts = [half_forward(group) for group in range(KV_HEADS)]
        running = tuple(jnp.stack(part) for part in zip(*parts))
    else:
        empty_max = jnp.full((KV_HEADS, group_size, row_count), MASKED_SCORE, jnp.float32)
        running = (
            empty_max,
            jnp.zeros((KV_HEADS, group_size, row_count), jnp.float32),
            jnp.zeros((KV_HEADS, group_size, row_count, HEAD_DIM), jnp.float32),
        )
        running = attend_block(running, own_block, own_start)

        def forward_turn(offset, carried):
            moving = passed_along(carried[1], "ctx", 1)
            return (attend_block(carried[0], moving, block_start(offset)), moving)

        running, last_moving = lax.fori_loop(
            1, half_blocks, forward_turn, (running, own_block)
        )
    maxima, totals, summed = running
    attention = summed / totals[..., None]
    log_totals = maxima + jnp.log(totals)
    attention_low = (
        attention.transpose(2, 0, 1, 3).reshape(row_count, HEADS * HEAD_DIM).astype(jnp.bfloat16)
    )
    residual = inputs + jnp.dot(attention_low, out_full, preferred_element_type=jnp.float32)
    scale_two = rms_scale(residual)
    gain_second = gain_two.astype(jnp.float32)
    normed_two = (residual * scale_two * gain_second).astype(jnp.bfloat16)
    gate_pre = jnp.dot(normed_two, gate_full, preferred_element_type=jnp.float32)
    up_pre = jnp.dot(normed_two, up_full, preferred_element_type=jnp.float32)
    gate_sigmoid = jax.nn.sigmoid(gate_pre)
    gate_silu = gate_pre * gate_sigmoid
    hidden_low = (gate_silu * up_pre).astype(jnp.bfloat16)
    output = (residual + jnp.dot(hidden_low, down_full, preferred_element_type=jnp.float32)).astype(
        jnp.bfloat16
    )
    grad_down = jnp.einsum("rf,rd->fd", hidden_low, cotangent, preferred_element_type=jnp.float32)
    grad_hidden = jnp.einsum("rd,fd->rf", cotangent, down_full, preferred_element_type=jnp.float32)
    grad_gate_low = (
        grad_hidden * up_pre * (gate_sigmoid * (1.0 + gate_pre * (1.0 - gate_sigmoid)))
    ).astype(jnp.bfloat16)
    grad_up_low = (grad_hidden * gate_silu).astype(jnp.bfloat16)
    grad_gate = jnp.einsum(
        "rd,rf->df", normed_two, grad_gate_low, preferred_element_type=jnp.float32
    )
    grad_up = jnp.einsum("rd,rf->df", normed_two, grad_up_low, preferred_element_type=jnp.float32)
    grad_normed_two = jnp.einsum(
        "rf,df->rd", grad_gate_low, gate_full, preferred_element_type=jnp.float32
    ) + jnp.einsum("rf,df->rd", grad_up_low, up_full, preferred_element_type=jnp.float32)
    grad_from_second, grad_gain_two = norm_back(grad_normed_two, residual, scale_two, gain_second)
    grad_residual = cotangent.astype(jnp.float32) + grad_from_second
    grad_branch = grad_residual.astype(jnp.bfloat16)
    grad_out = jnp.einsum(
        "rd,re->de", attention_low, grad_branch, preferred_element_type=jnp.float32
    )
    grad_attention = jnp.einsum(
        "re,de->rd", grad_branch, out_full, preferred_element_type=jnp.float32
    ).astype(jnp.bfloat16)
    grad_grid = grad_attention.reshape(row_count, KV_HEADS, group_size, HEAD_DIM).transpose(
        1, 2, 0, 3
    )
    row_dots = jnp.sum(grad_grid.astype(jnp.float32) * attention, axis=-1)

    def gradient_block(query_grads, kv_block, key_start):
        current = query_grads
        masked, key_rows, value_rows = scores_of(kv_block, key_start)
        probability = jnp.exp(masked - log_totals[..., None])
        grad_values = jnp.einsum(
            "girk,gird->kgd",
            probability.astype(jnp.bfloat16),
            grad_grid,
            preferred_element_type=jnp.float32,
        )
        grad_probability = jnp.einsum(
            "gird,kgd->girk", grad_grid, value_rows, preferred_element_type=jnp.float32
        )
        grad_scores = (probability * (grad_probability - row_dots[..., None])).astype(jnp.bfloat16)
        current = (
            current
            + jnp.einsum(
                "girk,kgd->gird", grad_scores, key_rows, preferred_element_type=jnp.float32
            )
            * score_scale
        )
        grad_keys = (
            jnp.einsum(
                "girk,gird->kgd", grad_scores, query_grid, preferred_element_type=jnp.float32
            )
            * score_scale
        )
        return (
            current,
            jnp.concatenate(
                [
                    grad_keys.reshape(block_rows, kv_width),
                    grad_values.reshape(block_rows, kv_width),
                ],
                axis=1,
            ),
        )

    def half_backward(group):
        masked = half_scores(group)
        probability = jnp.exp(masked - log_totals[group][..., None])
        grad_values = jnp.einsum(
            "irk,ird->kd",
            probability.astype(jnp.bfloat16),
            grad_grid[group],
            preferred_element_type=jnp.float32,
        )
        grad_probability = jnp.einsum(
            "ird,kd->irk",
            grad_grid[group],
            half_values[:, group],
            preferred_element_type=jnp.float32,
        )
        grad_scores = (probability * (grad_probability - row_dots[group][..., None])).astype(
            jnp.bfloat16
        )
        query_part = (
            jnp.einsum(
                "irk,kd->ird", grad_scores, half_keys[:, group], preferred_element_type=jnp.float32
            )
            * score_scale
        )
        grad_keys = (
            jnp.einsum(
                "irk,ird->kd", grad_scores, query_grid[group], preferred_element_type=jnp.float32
            )
            * score_scale
        )
        return (query_part, grad_keys.astype(jnp.bfloat16), grad_values.astype(jnp.bfloat16))

    if whole_half:
        parts = [half_backward(group) for group in range(KV_HEADS)]
        query_grads = jnp.stack([part[0] for part in parts])
        own_grads = lax.psum_scatter(
            jnp.concatenate([part[1] for part in parts] + [part[2] for part in parts], axis=1),
            ("ctx", "wa"),
            scatter_dimension=0,
            tiled=True,
            axis_index_groups=halves,
        ).astype(jnp.float32)
    else:
        query_grads, partial_value = gradient_block(
            jnp.zeros((KV_HEADS, group_size, row_count, HEAD_DIM), jnp.float32), own_block, own_start
        )

        def backward_turn(offset, carried):
            query_grads, moving, moving_grads = carried
            moving = passed_along(moving, "ctx", 1)
            moving_grads = shifted(moving_grads.astype(jnp.bfloat16), "ctx", 1).astype(
                moving_grads.dtype
            )
            query_grads, partial_value = gradient_block(query_grads, moving, block_start(offset))
            return (query_grads, moving, moving_grads + partial_value)

        query_grads, moving, moving_grads = lax.fori_loop(
            1, half_blocks, backward_turn, (query_grads, own_block, partial_value)
        )
        home_grads = shifted(moving_grads.astype(jnp.bfloat16), "ctx", 1 - half_blocks).astype(
            moving_grads.dtype
        )
        own_grads = lax.psum_scatter(
            home_grads.astype(jnp.bfloat16), "wa", scatter_dimension=0, tiled=True
        ).astype(jnp.float32)
    grad_key_rot = own_grads[:, :kv_width].reshape(row_count, KV_HEADS, HEAD_DIM)
    grad_key_low = (
        unrotate(grad_key_rot, cosine_table, sine_table)
        .reshape(row_count, kv_width)
        .astype(jnp.bfloat16)
    )
    grad_value_low = own_grads[:, kv_width:].astype(jnp.bfloat16)
    grad_query_rot = query_grads.transpose(2, 0, 1, 3).reshape(row_count, HEADS, HEAD_DIM)
    grad_query_low = (
        unrotate(grad_query_rot, cosine_table, sine_table)
        .reshape(row_count, HEADS * HEAD_DIM)
        .astype(jnp.bfloat16)
    )
    grad_query_w = jnp.einsum(
        "rd,re->de", normed, grad_query_low, preferred_element_type=jnp.float32
    )
    grad_key_w = jnp.einsum("rd,re->de", normed, grad_key_low, preferred_element_type=jnp.float32)
    grad_value_w = jnp.einsum(
        "rd,re->de", normed, grad_value_low, preferred_element_type=jnp.float32
    )
    grad_normed = jnp.einsum(
        "re,de->rd", grad_query_low, query_full, preferred_element_type=jnp.float32
    )
    grad_normed = grad_normed + jnp.einsum(
        "re,de->rd", grad_key_low, key_full, preferred_element_type=jnp.float32
    )
    grad_normed = grad_normed + jnp.einsum(
        "re,de->rd", grad_value_low, value_full, preferred_element_type=jnp.float32
    )
    grad_from_first, grad_gain_one = norm_back(grad_normed, inputs, scale_one, gain_first)
    grad_tokens = (grad_residual + grad_from_first).astype(jnp.bfloat16)

    def summed_grads(parts):
        joined = jnp.concatenate([part.astype(jnp.bfloat16) for part in parts], axis=1)
        owned = lax.psum_scatter(joined, "wa", scatter_dimension=0, tiled=True)
        return lax.psum(owned, "ctx").astype(jnp.float32)

    total_down = summed_grads([grad_down])
    total_late = summed_grads([grad_out, grad_gate, grad_up])
    total_early = summed_grads(
        [grad_query_w, grad_key_w, grad_value_w, grad_gain_one[:, None], grad_gain_two[:, None]]
    )
    return (
        output,
        grad_tokens,
        total_early[:, : ends[0]],
        total_early[:, ends[0] : ends[1]],
        total_early[:, ends[1] : ends[2]],
        total_late[:, : widths[3]],
        total_late[:, widths[3] : widths[3] + widths[4]],
        total_late[:, widths[3] + widths[4] :],
        total_down,
        total_early[:, ends[2]],
        total_early[:, ends[2] + 1],
    )


def solution(mesh):
    return jax.shard_map(
        on_device,
        mesh=mesh,
        in_specs=(
            P(("ctx", "wa"), None),
            P(),
            P("wa", None),
            P("wa", None),
            P("wa", None),
            P("wa", None),
            P("wa", None),
            P("wa", None),
            P("wa", None),
            P("wa"),
            P("wa"),
            P(("ctx", "wa"), None),
        ),
        out_specs=(
            P(("ctx", "wa"), None),
            P(("ctx", "wa"), None),
            P("wa", None),
            P("wa", None),
            P("wa", None),
            P("wa", None),
            P("wa", None),
            P("wa", None),
            P("wa", None),
            P("wa"),
            P("wa"),
        ),
        check_vma=False,
    )
```
